256 devices in a mesh: group: 4 (over x), tile: 64 (over z, y, core).
Axes of the slice: x: 4, y: 4, z: 8, core: 2. Of those that a mesh axis runs over, the one named last changes fastest.
Arguments:
- embeddings: bfloat16 [32768, 1024], P(('group', 'tile')), may hold values from -15 to 15
- row_group: int32 [32768, 1], P(('group', 'tile')), may hold values from 0 to 3, as said below
Outputs:
- max_similarity: float32 [32768], P(('group', 'tile'))
- soft_count: float32 [32768], P(('group', 'tile'))
The draws below stay inside these ranges and needn't reach their ends.
Inputs may be any that keep to these rules, and one draw needn't show every extreme that they name: `row_group`: among the rows of one storage shard (aligned blocks of 128 rows) at most 64 name the same cluster, some cluster is named by exactly 64 of them, and every cluster is named by at least one of them.
All inputs are finite; a program needn't handle non-finite values.
Results may differ from the reference program's by a relative error of at most 0.0003.
Values may be sent and summed in bfloat16 or wider, within the bound.
No kernel may reach another device: no remote copies, remote signals or barrier semaphores. Data moves between devices by JAX's collectives and lax.ppermute only.
A program may use at most 128 MiB of HBM per device.

```python
import math
import jax
import jax.numpy as jnp
from jax import lax

E = 1024
ROWS_DEV = 128
CAP = 64
BUF = 16384
TOTAL = 32768
N_GROUP = 4


def shard_groups(key):
    shards = TOTAL // ROWS_DEV
    rest = ROWS_DEV - CAP
    favored = jax.random.randint(jax.random.fold_in(key, 11), (), 0, N_GROUP)
    weights = jnp.arange(N_GROUP - 1, 0, -1, dtype=jnp.int32)
    bounds = jnp.cumsum(weights)
    whole = bounds[N_GROUP - 2]
    picks = jax.random.randint(jax.random.fold_in(key, 12), (shards, rest), 0, whole)
    shifted = jnp.sum((picks[:, :, None] >= bounds[None, None, :N_GROUP - 2]).astype(jnp.int32), axis=2)
    places = jnp.arange(rest, dtype=jnp.int32)[None, :]
    shifted = jnp.where(places < N_GROUP - 1, places, shifted)
    others = (favored + 1 + shifted) % N_GROUP
    leading = jnp.full((shards, CAP), favored, jnp.int32)
    layout = jnp.concatenate([leading, others.astype(jnp.int32)], axis=1)
    keys = jax.random.split(jax.random.fold_in(key, 14), shards)
    orders = jax.vmap(lambda k: jax.random.permutation(k, ROWS_DEV))(keys)
    mixed = jnp.take_along_axis(layout, orders.astype(jnp.int32), axis=1)
    return mixed.reshape(TOTAL).astype(jnp.int32)


def draw_row_group(key, part):
    groups = shard_groups(key)
    return groups.reshape(TOTAL, 1)


def draw_embeddings(key, part):
    groups = shard_groups(key)
    families_each = max(1, TOTAL // (6 * N_GROUP))
    family = groups * families_each + jax.random.randint(jax.random.fold_in(key, 13), (TOTAL,), 0, families_each)
    key = jax.random.fold_in(key, 5)
    keys = jax.random.split(key, 3)
    base = jnp.clip(jax.random.normal(keys[0], (N_GROUP * families_each, E), jnp.float32), -4.0, 4.0)
    mix = jax.random.uniform(keys[1], (TOTAL, 1), jnp.float32, 0.2, 0.95)
    spread = math.sqrt(12.0 / math.sqrt(E))
    noise = jnp.clip(jax.random.normal(keys[2], (TOTAL, E), jnp.float32), -4.0, 4.0)
    factor = spread
    rows = factor * (mix * base[family] + jnp.sqrt(1.0 - mix * mix) * noise)
    return rows.astype(jnp.bfloat16)


def setup_inputs(seed: int = 0) -> dict:
    arg_keys = jax.random.split(jax.random.key(seed), 3)
    embeddings = draw_embeddings(jax.random.fold_in(arg_keys[2], 71), 0)
    row_group = draw_row_group(jax.random.fold_in(arg_keys[2], 71), 0)
    return {"embeddings": embeddings, "row_group": row_group}


def group_stats(rows, valid, block):
    scale = 1.0 / math.sqrt(E)
    length = rows.shape[0]
    places = jnp.arange(length, dtype=jnp.int32)
    starts = jnp.arange(0, length, block, dtype=jnp.int32)

    def one_block(start):
        query = lax.dynamic_slice_in_dim(rows, start, block, 0)
        query_valid = lax.dynamic_slice_in_dim(valid, start, block, 0)
        query_places = start + jnp.arange(block, dtype=jnp.int32)
        score = jnp.dot(query, rows.T, preferred_element_type=jnp.float32) * scale
        same = query_valid[:, None] & valid[None, :] & (query_places[:, None] != places[None, :])
        top = lax.optimization_barrier(jnp.max(jnp.where(same, score, -1e+30), axis=1))
        total = lax.optimization_barrier(jnp.sum(jnp.where(same, jnp.exp(score - 3.0), 0.0), axis=1))
        return (top, total)
    top, total = lax.map(one_block, starts)
    return (top.reshape(length), total.reshape(length))

def reference(embeddings, row_group):
    groups = row_group[:, 0]
    block = math.gcd(BUF, 1024)
    best_out = jnp.zeros((TOTAL,), jnp.float32)
    soft_out = jnp.zeros((TOTAL,), jnp.float32)
    for g in range(N_GROUP):
        flag = jnp.where(groups == g, 0, 1).astype(jnp.int32)
        order = jnp.argsort(flag, stable=True)[:BUF].astype(jnp.int32)
        valid = groups[order] == g
        rows = embeddings[order]
        top, total = group_stats(rows, valid, block)
        target = jnp.where(valid, order, TOTAL).astype(jnp.int32)
        best_out = best_out.at[target].set(top, mode='drop')
        soft_out = soft_out.at[target].set(jnp.log1p(total), mode='drop')
    return (best_out, soft_out)
```

```python
import functools
import math

import jax
import jax.numpy as jnp
from jax import lax
from jax.experimental import pallas as pl
from jax.experimental.pallas import tpu as pltpu
from jax.sharding import Mesh, PartitionSpec as P

NX, NZ, NY, NC = 4, 8, 4, 2
AXES = ("x", "z", "y", "c")
ROWS = 128
WIDTH = 1024
PAIR = 2 * ROWS
EXTRA = 16
SLOT = ROWS + EXTRA
CHUNK = PAIR + EXTRA
LOWEST = -1e30
SCALE = 1.0 / math.sqrt(WIDTH)
LOG2E = math.log2(math.e)
OFFSET = 3.0
ANY = pl.BlockSpec(memory_space=pl.ANY)
VM = pl.BlockSpec(memory_space=pltpu.VMEM)
SM = pl.BlockSpec(memory_space=pltpu.SMEM)


def device_index(x, z, y, c):
    return (((x % NX) * NZ + z % NZ) * NY + y % NY) * NC + c


def shift(value, move):
    pairs = []
    for x in range(NX):
        for z in range(NZ):
            for y in range(NY):
                for c in range(NC):
                    dx, dz, dy, dc = move(c)
                    target = device_index(x + dx, z + dz, y + dy, (c + dc) % NC)
                    pairs.append((device_index(x, z, y, c), target))
    return lax.ppermute(value, AXES, pairs)


def swap(value):
    return shift(value, lambda c: (0, 0, 0, 1))


def along_z(value):
    return shift(value, lambda c: (0, 1, 0, 0) if c == 0 else (0, -1, 0, 0))


def first_axis(value, step):
    return shift(value, lambda c: (step, 0, 0, 0) if c == 0 else (0, 0, step, 0))


def second_axis(value, step):
    return shift(value, lambda c: (0, 0, step, 0) if c == 0 else (step, 0, 0, 0))


def bf16(*shape):
    return jax.ShapeDtypeStruct(shape, jnp.bfloat16)


def f32(*shape):
    return jax.ShapeDtypeStruct(shape, jnp.float32)


def prepare_kernel(rows_ref, mark_ref, out_ref):
    out_ref[0:ROWS, :] = rows_ref[...]
    wide = jnp.broadcast_to(mark_ref[...].astype(jnp.float32), (ROWS, 128))
    for g in range(0, 8, 2):
        lane = lax.broadcasted_iota(jnp.int32, (16, 128), 1)
        both = jnp.where(lane < 64, wide[16 * g : 16 * g + 16], wide[16 * g + 16 : 16 * g + 32])
        out_ref[ROWS:SLOT, 64 * g : 64 * g + 128] = both.astype(jnp.bfloat16)
    out_ref[ROWS:SLOT, 512:640] = wide.T[0:16].astype(jnp.bfloat16)
    out_ref[ROWS:SLOT, 640:] = jnp.zeros((16, WIDTH - 640), jnp.bfloat16)


def prepare(rows, mark):
    return pl.pallas_call(
        prepare_kernel, out_shape=bf16(SLOT, WIDTH), in_specs=[VM, VM], out_specs=VM, name="prepare"
    )(rows, mark)


def pack_keys_kernel(a_ref, b_ref, out_ref):
    out_ref[0:ROWS] = a_ref[0:ROWS]
    out_ref[ROWS:PAIR] = b_ref[0:ROWS]
    out_ref[PAIR:, 0:512] = a_ref[ROWS:, 0:512]
    out_ref[PAIR:, 512:] = b_ref[ROWS:, 0:512]


def pack_queries_kernel(a_ref, b_ref, out_ref):
    out_ref[0:ROWS] = a_ref[0:ROWS]
    out_ref[ROWS:PAIR] = b_ref[0:ROWS]
    out_ref[PAIR:, 0:128] = a_ref[ROWS:, 512:640]
    out_ref[PAIR:, 128:256] = b_ref[ROWS:, 512:640]
    out_ref[PAIR:, 256:] = jnp.zeros((EXTRA, WIDTH - 256), jnp.bfloat16)


def pack(kernel, a, b, name):
    return pl.pallas_call(
        kernel, out_shape=bf16(CHUNK, WIDTH), in_specs=[VM, VM], out_specs=VM, name=name
    )(a, b)


def stage_kernel(key_rows, n_query, own, *refs):
    n_key = len(key_rows)
    q_refs, k_refs = refs[:n_query], refs[n_query : n_query + n_key]
    top_ref, total_ref, q_buf, k_buf, mark_buf, column, q_sem, k_sem, m_sem = refs[n_query + n_key :]
    starts = [sum(key_rows[:i]) for i in range(n_key)]
    length = sum(key_rows)

    copies = []
    for i in range(n_query):
        copies.append(pltpu.make_async_copy(q_refs[i], q_buf.at[i], q_sem.at[i]))
    for i, rows in enumerate(key_rows):
        copies.append(
            pltpu.make_async_copy(
                k_refs[i].at[pl.ds(0, rows)], k_buf.at[pl.ds(starts[i], rows)], k_sem.at[i]
            )
        )
        copies.append(
            pltpu.make_async_copy(k_refs[i].at[pl.ds(rows, EXTRA)], mark_buf.at[i], m_sem.at[i])
        )
    for copy in copies:
        copy.start()
    for copy in copies:
        copy.wait()

    for i, rows in enumerate(key_rows):
        for g in range(rows // 16):
            lane = 64 * (g if rows == PAIR else g + 8)
            values = mark_buf[i, :, lane : lane + 1].astype(jnp.float32)
            column[pl.ds(starts[i] + 16 * g, 16), :] = jnp.broadcast_to(values, (16, 128))

    def block(q, start, carry, diagonal):
        score = lax.dot_general(
            k_buf[pl.ds(start, PAIR), :],
            q_buf[q, 0:PAIR, :],
            (((1,), (1,)), ((), ())),
            preferred_element_type=jnp.float32,
        )
        column_mark = column[pl.ds(start, PAIR), :]
        marks = q_buf[q, PAIR:CHUNK, 0:256].astype(jnp.float32)[0:1]
        tops, totals = [], []
        for half in range(2):
            part = score[:, 128 * half : 128 * half + 128]
            same = column_mark == marks[:, 128 * half : 128 * half + 128]
            if diagonal and half == 0:
                row = lax.broadcasted_iota(jnp.int32, (PAIR, 128), 0)
                lane = lax.broadcasted_iota(jnp.int32, (PAIR, 128), 1)
                same = same & (row != lane)
            part = jnp.where(same, part, LOWEST)
            weight = jnp.exp2(part * (SCALE * LOG2E) - OFFSET * LOG2E)
            tops.append(jnp.max(part.reshape(PAIR // 8, 8, 128), 0))
            totals.append(jnp.sum(weight.reshape(PAIR // 8, 8, 128), 0))
        top, total = carry
        return (
            jnp.maximum(top, jnp.concatenate(tops, 1)),
            total + jnp.concatenate(totals, 1),
        )

    empty = (jnp.full((8, PAIR), LOWEST, jnp.float32), jnp.zeros((8, PAIR), jnp.float32))

    def query(q, first, carry):
        def body(k, carry):
            return block(q, pl.multiple_of(k * PAIR, PAIR), carry, False)

        carry = lax.fori_loop(first, length // PAIR, body, carry)
        top_ref[q], total_ref[q] = carry

    if own:
        query(0, 1, block(0, 0, empty, True))

    def outer(q, _):
        query(q, 0, empty)
        return 0

    lax.fori_loop(1 if own else 0, n_query, outer, 0)


def stage(queries, keys, own, name):
    n_query, n_key = len(queries), len(keys)
    key_rows = tuple(k.shape[0] - EXTRA for k in keys)
    length = sum(key_rows)
    return pl.pallas_call(
        functools.partial(stage_kernel, key_rows, n_query, own),
        out_shape=(f32(n_query, 8, PAIR), f32(n_query, 8, PAIR)),
        in_specs=[ANY] * (n_query + n_key),
        out_specs=(VM, VM),
        scratch_shapes=[
            pltpu.VMEM((n_query, CHUNK, WIDTH), jnp.bfloat16),
            pltpu.VMEM((length, WIDTH), jnp.bfloat16),
            pltpu.VMEM((n_key, EXTRA, WIDTH), jnp.bfloat16),
            pltpu.VMEM((length, 128), jnp.float32),
            pltpu.SemaphoreType.DMA((n_query,)),
            pltpu.SemaphoreType.DMA((n_key,)),
            pltpu.SemaphoreType.DMA((n_key,)),
        ],
        compiler_params=pltpu.CompilerParams(vmem_limit_bytes=24 << 20),
        cost_estimate=pl.CostEstimate(
            flops=2 * n_query * PAIR * length * WIDTH,
            bytes_accessed=2 * (n_query * PAIR + length) * WIDTH,
            transcendentals=n_query * PAIR * length,
        ),
        name=name,
    )(*queries, *keys)


def collect_kernel(plan, place_ref, *refs):
    out_ref = refs[-1]
    for chunk, sources in enumerate(plan):
        top = functools.reduce(jnp.maximum, [refs[2 * s][i] for s, i in sources])
        total = functools.reduce(jnp.add, [refs[2 * s + 1][i] for s, i in sources])
        top = jnp.max(top, 0, keepdims=True)
        total = jnp.sum(total, 0, keepdims=True)
        for half in range(2):
            place = place_ref[2 * chunk + half] * 2
            out_ref[pl.ds(place, 1), :] = top[:, 128 * half : 128 * half + 128]
            out_ref[pl.ds(place + 1, 1), :] = total[:, 128 * half : 128 * half + 128]


def collect(plan, places, stages):
    flat = [a for pair in stages for a in pair]
    return pl.pallas_call(
        functools.partial(collect_kernel, plan),
        out_shape=f32(2 * NX * NY, 128),
        in_specs=[SM] + [VM] * len(flat),
        out_specs=VM,
        name="collect",
    )(places, *flat)


def finish_kernel(parts_ref, top_ref, soft_ref):
    top = parts_ref[0:1, :]
    total = parts_ref[1:2, :]
    for i in range(1, NX * NY):
        top = jnp.maximum(top, parts_ref[2 * i : 2 * i + 1, :])
        total = total + parts_ref[2 * i + 1 : 2 * i + 2, :]
    top_ref[...] = top * SCALE
    soft_ref[...] = jnp.log1p(total)


def finish(parts):
    return pl.pallas_call(
        finish_kernel, out_shape=(f32(1, ROWS), f32(1, ROWS)), in_specs=[VM], out_specs=(VM, VM), name="finish"
    )(parts)


def per_device(rows, mark):
    mine = prepare(rows, mark)
    other = swap(mine)
    a = first_axis(mine, 1)
    b = first_axis(mine, -1)
    z0 = pack(pack_keys_kernel, mine, other, "pack_keys")
    t1 = along_z(z0)
    x1 = pack(pack_queries_kernel, mine, a, "pack_near")
    d = first_axis(a, 1)
    e1 = second_axis(x1, 1)
    f1 = second_axis(x1, -1)
    x2 = pack(pack_queries_kernel, b, d, "pack_far")
    t2 = along_z(t1)
    u1 = swap(t1)
    e2 = second_axis(x2, 1)
    f2 = second_axis(x2, -1)
    t3 = along_z(t2)
    u2 = swap(t2)
    g1 = second_axis(e1, 1)
    g2 = second_axis(f2, -1)
    t4 = along_z(t3[ROWS:])
    u3 = swap(t3)
    u4 = swap(t4)

    s1 = stage([x1, x2], [z0, t1, u1], True, "stage_own")
    s2 = stage([x1, x2], [t2, u2, t3, u3], False, "stage_keys")
    s3 = stage([e1, f1, e2, f2], [z0, t1, u1, t2, u2, t3, u3], False, "stage_queries")
    s4 = stage([x1, x2, e1, f1, e2, f2], [t4, u4], False, "stage_last_keys")
    s5 = stage([g1, g2], [z0, t1, u1, t2, u2, t3, u3, t4, u4], False, "stage_last_queries")

    near, far = ((0, 0), (-1, 0)), ((1, 0), (-2, 0))
    move = lambda pair, step: tuple((p, step) for p, _ in pair)
    chunks = [near, far, move(near, -1), move(near, 1), move(far, -1), move(far, 1), move(near, -2), move(far, 2)]
    plan = [[(0, 0), (1, 0), (3, 0)], [(0, 1), (1, 1), (3, 1)]]
    plan += [[(2, i), (3, i + 2)] for i in range(4)]
    plan += [[(4, i)] for i in range(2)]
    steps = jnp.array([s for pair in chunks for s in pair], jnp.int32)
    core = lax.axis_index("c")
    first, second = steps[:, 0], steps[:, 1]
    dx = jnp.where(core == 0, first, second)
    dy = jnp.where(core == 0, second, first)
    px = (lax.axis_index("x") + dx + NX) % NX
    py = (lax.axis_index("y") + dy + NY) % NY
    places = px * NY + py

    parts = collect(plan, places, [s1, s2, s3, s4, s5])
    parts = lax.all_to_all(parts, ("x", "y"), split_axis=0, concat_axis=0, tiled=True)
    top, soft = finish(parts)
    return top.reshape(ROWS), soft.reshape(ROWS)


def solution(mesh):
    fine = Mesh(mesh.devices.reshape(NX, NZ, NY, NC), AXES)
    return jax.shard_map(
        per_device,
        mesh=fine,
        in_specs=(P(AXES, None), P(AXES, None)),
        out_specs=(P(AXES), P(AXES)),
        check_vma=False,
    )
```

```python
import functools
import math

import jax
import jax.numpy as jnp
from jax import lax
from jax.experimental import pallas as pl
from jax.experimental.pallas import tpu as pltpu
from jax.sharding import Mesh, PartitionSpec as P

NX, NZ, NY, NC = 4, 8, 4, 2
AXES = ("x", "z", "y", "c")
ROWS = 128
WIDTH = 1024
PAIR = 2 * ROWS
EXTRA = 16
SLOT = ROWS + EXTRA
CHUNK = PAIR + EXTRA
LOWEST = -1e30
SCALE = 1.0 / math.sqrt(WIDTH)
LOG2E = math.log2(math.e)
OFFSET = 3.0
VM = pl.BlockSpec(memory_space=pltpu.VMEM)
SMALL = pltpu.CompilerParams(vmem_limit_bytes=4 << 20)


def device_index(x, z, y, c):
    return (((x % NX) * NZ + z % NZ) * NY + y % NY) * NC + c


def shift(value, move):
    pairs = []
    for x in range(NX):
        for z in range(NZ):
            for y in range(NY):
                for c in range(NC):
                    dx, dz, dy, dc = move(c)
                    target = device_index(x + dx, z + dz, y + dy, (c + dc) % NC)
                    pairs.append((device_index(x, z, y, c), target))
    return lax.ppermute(value, AXES, pairs)


def swap(value):
    return shift(value, lambda c: (0, 0, 0, 1))


def along_z(value, step):
    return shift(value, lambda c: (0, step, 0, 0))


def away(value):
    return shift(value, lambda c: (0, 1, 0, 0) if c == 0 else (0, -1, 0, 0))


def first_axis(value, step):
    return shift(value, lambda c: (step, 0, 0, 0) if c == 0 else (0, 0, step, 0))


def second_axis(value, step):
    return shift(value, lambda c: (0, 0, step, 0) if c == 0 else (step, 0, 0, 0))


def bf16(*shape):
    return jax.ShapeDtypeStruct(shape, jnp.bfloat16)


def f32(*shape):
    return jax.ShapeDtypeStruct(shape, jnp.float32)


def prepare_kernel(rows_ref, mark_ref, out_ref):
    out_ref[0:ROWS, :] = rows_ref[...]
    along = jnp.broadcast_to(mark_ref[...].astype(jnp.float32), (ROWS, 128))
    wide = along.T
    lane = lax.broadcasted_iota(jnp.int32, (16, 128), 1)
    for g in range(0, 8, 2):
        both = jnp.where(lane < 64, wide[16 * g : 16 * g + 16], wide[16 * g + 16 : 16 * g + 32])
        out_ref[ROWS:SLOT, 64 * g : 64 * g + 128] = both.astype(jnp.bfloat16)
    out_ref[ROWS:SLOT, 512:640] = along[0:16].astype(jnp.bfloat16)
    out_ref[ROWS:SLOT, 640:] = jnp.zeros((16, WIDTH - 640), jnp.bfloat16)


def prepare(rows, mark):
    return pl.pallas_call(
        prepare_kernel,
        out_shape=bf16(SLOT, WIDTH),
        in_specs=[VM, VM],
        out_specs=VM,
        compiler_params=SMALL,
        name="prepare",
    )(rows, mark.reshape(1, ROWS))


def pack_keys_kernel(a_ref, b_ref, out_ref):
    out_ref[0:ROWS] = a_ref[0:ROWS]
    out_ref[ROWS:PAIR] = b_ref[0:ROWS]
    out_ref[PAIR:, 0:512] = a_ref[ROWS:, 0:512]
    out_ref[PAIR:, 512:] = b_ref[ROWS:, 0:512]


def pack_far_keys_kernel(low_ref, low_other_ref, high_ref, high_other_ref, out_ref):
    @pl.when(lax.axis_index("c") == 0)
    def _():
        pack_keys_kernel(low_ref, low_other_ref, out_ref)

    @pl.when(lax.axis_index("c") != 0)
    def _():
        pack_keys_kernel(high_ref, high_other_ref, out_ref)


def second_half_kernel(keys_ref, out_ref):
    out_ref[...] = keys_ref[ROWS:]


def second_half(keys):
    return pl.pallas_call(
        second_half_kernel,
        out_shape=bf16(SLOT, WIDTH),
        in_specs=[VM],
        out_specs=VM,
        compiler_params=SMALL,
        name="second_half",
    )(keys)


def pack_queries_kernel(a_ref, b_ref, out_ref):
    out_ref[0:ROWS] = a_ref[0:ROWS]
    out_ref[ROWS:PAIR] = b_ref[0:ROWS]
    out_ref[PAIR:, 0:128] = a_ref[ROWS:, 512:640]
    out_ref[PAIR:, 128:256] = b_ref[ROWS:, 512:640]
    out_ref[PAIR:, 256:] = jnp.zeros((EXTRA, WIDTH - 256), jnp.bfloat16)


def pack(kernel, name, *parts):
    return pl.pallas_call(
        kernel,
        out_shape=bf16(CHUNK, WIDTH),
        in_specs=[VM] * len(parts),
        out_specs=VM,
        compiler_params=SMALL,
        name=name,
    )(*parts)


def stage_kernel(key_rows, n_query, work, own, *refs):
    n_key = len(key_rows)
    q_refs, k_refs = refs[:n_query], refs[n_query : n_query + n_key]
    out_ref, column = refs[n_query + n_key :]

    for i, rows in enumerate(key_rows):
        for g in range(rows // 16):
            lane = 64 * (g if rows == PAIR else g + 8)
            values = k_refs[i][rows : rows + EXTRA, lane : lane + 1].astype(jnp.float32)
            column[i, 16 * g : 16 * g + 16, :] = jnp.broadcast_to(values, (16, 128))

    for q, keys in enumerate(work):
        marks = q_refs[q][PAIR:CHUNK, 0:PAIR].astype(jnp.float32)[0:1]
        top = jnp.full((8, PAIR), LOWEST, jnp.float32)
        total = jnp.zeros((8, PAIR), jnp.float32)
        for k in keys:
            rows = key_rows[k]
            score = lax.dot_general(
                k_refs[k][0:rows, :],
                q_refs[q][0:PAIR, :],
                (((1,), (1,)), ((), ())),
                preferred_element_type=jnp.float32,
            )
            column_mark = column[k, 0:rows, :]
            tops, totals = [], []
            for half in range(2):
                part = score[:, 128 * half : 128 * half + 128]
                same = column_mark == marks[:, 128 * half : 128 * half + 128]
                if own and q == 0 and k == 0 and half == 0:
                    row = lax.broadcasted_iota(jnp.int32, (rows, 128), 0)
                    lane = lax.broadcasted_iota(jnp.int32, (rows, 128), 1)
                    same = same & (row != lane)
                part = jnp.where(same, part, LOWEST)
                weight = jnp.exp2(part * (SCALE * LOG2E) - OFFSET * LOG2E)
                tops.append(jnp.max(part.reshape(rows // 8, 8, 128), 0))
                totals.append(jnp.sum(weight.reshape(rows // 8, 8, 128), 0))
            top = jnp.maximum(top, jnp.concatenate(tops, 1))
            total = total + jnp.concatenate(totals, 1)
        out_ref[q, 0:8] = top
        out_ref[q, 8:16] = total


def stage(queries, keys, work, own, name):
    n_query, n_key = len(queries), len(keys)
    key_rows = tuple(k.shape[0] - EXTRA for k in keys)
    pairs = PAIR * sum(key_rows[k] for each in work for k in each)
    return pl.pallas_call(
        functools.partial(stage_kernel, key_rows, n_query, work, own),
        out_shape=f32(n_query, 16, PAIR),
        in_specs=[VM] * (n_query + n_key),
        out_specs=VM,
        scratch_shapes=[pltpu.VMEM((n_key, PAIR, 128), jnp.float32)],
        compiler_params=pltpu.CompilerParams(vmem_limit_bytes=8 << 20),
        cost_estimate=pl.CostEstimate(
            flops=2 * pairs * WIDTH,
            bytes_accessed=2 * (n_query * PAIR + sum(key_rows)) * WIDTH,
            transcendentals=pairs,
        ),
        name=name,
    )(*queries, *keys)


def collect_kernel(plan, steps, *refs):
    out_ref = refs[-1]
    straight = lax.axis_index("c") == 0
    x, y = lax.axis_index("x"), lax.axis_index("y")
    for chunk, sources in enumerate(plan):
        top = functools.reduce(jnp.maximum, [refs[s][i, 0:8] for s, i in sources])
        total = functools.reduce(jnp.add, [refs[s][i, 8:16] for s, i in sources])
        top = jnp.max(top, 0, keepdims=True)
        total = jnp.sum(total, 0, keepdims=True)
        for half in range(2):
            first, second = steps[2 * chunk + half]
            to_x = lax.rem(x + jnp.where(straight, first, second) + NX, NX)
            to_y = lax.rem(y + jnp.where(straight, second, first) + NY, NY)
            place = (to_x * NY + to_y) * 2
            out_ref[pl.ds(place, 1), :] = top[:, 128 * half : 128 * half + 128]
            out_ref[pl.ds(place + 1, 1), :] = total[:, 128 * half : 128 * half + 128]


def collect(plan, steps, stages):
    return pl.pallas_call(
        functools.partial(collect_kernel, plan, steps),
        out_shape=f32(2 * NX * NY, 128),
        in_specs=[VM] * len(stages),
        out_specs=VM,
        compiler_params=SMALL,
        name="collect",
    )(*stages)


def finish_kernel(parts_ref, top_ref, soft_ref):
    top = parts_ref[0:1, :]
    total = parts_ref[1:2, :]
    for i in range(1, NX * NY):
        top = jnp.maximum(top, parts_ref[2 * i : 2 * i + 1, :])
        total = total + parts_ref[2 * i + 1 : 2 * i + 2, :]
    top_ref[...] = top * SCALE
    soft_ref[...] = jnp.log1p(total)


def finish(parts):
    return pl.pallas_call(
        finish_kernel,
        out_shape=(f32(1, ROWS), f32(1, ROWS)),
        in_specs=[VM],
        out_specs=(VM, VM),
        compiler_params=SMALL,
        name="finish",
    )(parts)


def per_device(rows, mark):
    together = lax.optimization_barrier
    mine = prepare(rows, mark)
    low = along_z(mine, 1)
    high = along_z(mine, -1)
    a = first_axis(mine, 1)
    b = first_axis(mine, -1)
    other = swap(mine)
    z0 = pack(pack_keys_kernel, "pack_keys", mine, other)
    low, high, a, b, z0 = together((low, high, a, b, z0))

    low_other = swap(low)
    high_other = swap(high)
    x1 = pack(pack_queries_kernel, "pack_near", mine, a)
    e1 = second_axis(x1, 1)
    f1 = second_axis(x1, -1)
    d = first_axis(a, 1)
    k1 = pack(pack_far_keys_kernel, "pack_far_keys", low, low_other, high, high_other)
    t2 = away(k1)
    zl = pack(pack_keys_kernel, "pack_low", low, low_other)
    zh = pack(pack_keys_kernel, "pack_high", high, high_other)
    s1 = stage([x1], [z0, zl, zh], ((0, 1, 2),), True, "stage_1")
    t2, e1, f1, d, s1, zl, zh = together((t2, e1, f1, d, s1, zl, zh))

    t3 = away(t2)
    u2 = swap(t2)
    x2 = pack(pack_queries_kernel, "pack_far", b, d)
    e2 = second_axis(x2, 1)
    f2 = second_axis(x2, -1)
    s2 = stage([x1, e1, f1], [z0, zl, zh, t2], ((3,), (0, 1, 2, 3), (0, 1, 2, 3)), False, "stage_2")
    t3, u2, e2, f2, s2 = together((t3, u2, e2, f2, s2))

    t4 = away(second_half(t3))
    u3 = swap(t3)
    g1 = second_axis(e1, 1)
    g2 = second_axis(f2, -1)
    s3 = stage(
        [x1, e1, f1, x2, e2, f2],
        [z0, zl, zh, t2, u2, t3],
        ((4, 5),) * 3 + ((0, 1, 2, 3, 4, 5),) * 3,
        False,
        "stage_3",
    )
    t4, u3, g1, g2, s3 = together((t4, u3, g1, g2, s3))

    u4 = swap(t4)
    s4 = stage(
        [x1, e1, f1, x2, e2, f2, g1, g2],
        [u3, t4, z0, zl, zh, t2, u2, t3],
        ((0, 1),) * 6 + ((0, 1, 2, 3, 4, 5, 6, 7),) * 2,
        False,
        "stage_4",
    )
    s5 = stage([x1, e1, f1, x2, e2, f2, g1, g2], [u4], ((0,),) * 8, False, "stage_5")

    near, far = ((0, 0), (-1, 0)), ((1, 0), (-2, 0))
    move = lambda pair, step: tuple((p, step) for p, _ in pair)
    chunks = [near, move(near, -1), move(near, 1), far, move(far, -1), move(far, 1), move(near, -2), move(far, 2)]
    steps = [s for pair in chunks for s in pair]
    stages = [s1, s2, s3, s4, s5]
    held = [(0,), (0, 1, 2), (0, 1, 2, 3, 4, 5), range(8), range(8)]
    plan = [[(s, q) for s in range(5) if q in held[s]] for q in range(8)]

    parts = collect(plan, steps, stages)
    parts = lax.all_to_all(parts, ("x", "y"), split_axis=0, concat_axis=0, tiled=True)
    top, soft = finish(parts)
    return top.reshape(ROWS), soft.reshape(ROWS)


def solution(mesh):
    fine = Mesh(mesh.devices.reshape(NX, NZ, NY, NC), AXES)
    return jax.shard_map(
        per_device,
        mesh=fine,
        in_specs=(P(AXES, None), P(AXES, None)),
        out_specs=(P(AXES), P(AXES)),
        check_vma=False,
    )
```

```python
import functools
import math

import jax
import jax.numpy as jnp
from jax import lax
from jax.experimental import pallas as pl
from jax.experimental.pallas import tpu as pltpu
from jax.sharding import Mesh, PartitionSpec as P

NX, NZ, NY, NC = 4, 8, 4, 2
AXES = ("x", "z", "y", "c")
ROWS = 128
WIDTH = 1024
PAIR = 2 * ROWS
EXTRA = 16
SLOT = ROWS + EXTRA
CHUNK = PAIR + EXTRA
LOWEST = -1e30
SCALE = 1.0 / math.sqrt(WIDTH)
LOG2E = math.log2(math.e)
OFFSET = 3.0
VM = pl.BlockSpec(memory_space=pltpu.VMEM)
SMALL = pltpu.CompilerParams(vmem_limit_bytes=4 << 20)


def device_index(x, z, y, c):
    return (((x % NX) * NZ + z % NZ) * NY + y % NY) * NC + c


def shift(value, move):
    pairs = []
    for x in range(NX):
        for z in range(NZ):
            for y in range(NY):
                for c in range(NC):
                    dx, dz, dy, dc = move(c)
                    target = device_index(x + dx, z + dz, y + dy, (c + dc) % NC)
                    pairs.append((device_index(x, z, y, c), target))
    return lax.ppermute(value, AXES, pairs)


def swap(value):
    return shift(value, lambda c: (0, 0, 0, 1))


def along_z(value, step):
    return shift(value, lambda c: (0, step, 0, 0))


def away(value, step=1):
    return shift(value, lambda c: (0, step, 0, 0) if c == 0 else (0, -step, 0, 0))


def first_axis(value, step):
    return shift(value, lambda c: (step, 0, 0, 0) if c == 0 else (0, 0, step, 0))


def second_axis(value, step):
    return shift(value, lambda c: (0, 0, step, 0) if c == 0 else (step, 0, 0, 0))


def bf16(*shape):
    return jax.ShapeDtypeStruct(shape, jnp.bfloat16)


def f32(*shape):
    return jax.ShapeDtypeStruct(shape, jnp.float32)


def prepare_kernel(rows_ref, mark_ref, out_ref, sem):
    copy = pltpu.make_async_copy(rows_ref, out_ref.at[pl.ds(0, ROWS)], sem)
    copy.start()
    along = jnp.broadcast_to(mark_ref[...].astype(jnp.float32), (ROWS, 128))
    wide = along.T
    lane = lax.broadcasted_iota(jnp.int32, (16, 128), 1)
    for g in range(0, 8, 2):
        both = jnp.where(lane < 64, wide[16 * g : 16 * g + 16], wide[16 * g + 16 : 16 * g + 32])
        out_ref[ROWS:SLOT, 64 * g : 64 * g + 128] = both.astype(jnp.bfloat16)
    out_ref[ROWS:SLOT, 512:640] = along[0:16].astype(jnp.bfloat16)
    out_ref[ROWS:SLOT, 640:] = jnp.zeros((16, WIDTH - 640), jnp.bfloat16)
    copy.wait()


def prepare(rows, mark):
    return pl.pallas_call(
        prepare_kernel,
        out_shape=bf16(SLOT, WIDTH),
        in_specs=[pl.BlockSpec(memory_space=pl.ANY), VM],
        out_specs=VM,
        scratch_shapes=[pltpu.SemaphoreType.DMA],
        compiler_params=SMALL,
        name="prepare",
    )(rows, mark.reshape(1, ROWS))


def pack_keys_kernel(a_ref, b_ref, out_ref):
    out_ref[0:ROWS] = a_ref[0:ROWS]
    out_ref[ROWS:PAIR] = b_ref[0:ROWS]
    out_ref[PAIR:, 0:512] = a_ref[ROWS:, 0:512]
    out_ref[PAIR:, 512:] = b_ref[ROWS:, 0:512]


def pack_queries_kernel(*refs):
    out_ref = refs[-1]
    last = ROWS * (len(refs) - 1)
    for i, ref in enumerate(refs[:-1]):
        out_ref[ROWS * i : ROWS * (i + 1)] = ref[0:ROWS]
        out_ref[last:, 128 * i : 128 * i + 128] = ref[ROWS:, 512:640]
    out_ref[last:, last:] = jnp.zeros((EXTRA, WIDTH - last), jnp.bfloat16)


def half_queries_kernel(half, whole_ref, out_ref):
    out_ref[0:PAIR] = whole_ref[PAIR * half : PAIR * half + PAIR]
    out_ref[PAIR:, 0:PAIR] = whole_ref[2 * PAIR :, PAIR * half : PAIR * half + PAIR]
    out_ref[PAIR:, PAIR:] = jnp.zeros((EXTRA, WIDTH - PAIR), jnp.bfloat16)


def pack(kernel, name, rows, *parts):
    return pl.pallas_call(
        kernel,
        out_shape=bf16(rows + EXTRA, WIDTH),
        in_specs=[VM] * len(parts),
        out_specs=VM,
        compiler_params=SMALL,
        name=name,
    )(*parts)


def stage_kernel(key_rows, chunk_counts, work, own, *refs):
    n_key, n_query = len(key_rows), len(chunk_counts)
    q_refs, k_refs = refs[:n_query], refs[n_query : n_query + n_key]
    out_ref, column = refs[n_query + n_key :]

    for i, rows in enumerate(key_rows):
        for g in range(rows // 16):
            lane = 64 * (g if rows == PAIR else g + 8)
            values = k_refs[i][rows : rows + EXTRA, lane : lane + 1].astype(jnp.float32)
            column[i, 16 * g : 16 * g + 16, :] = jnp.broadcast_to(values, (16, 128))

    places = [(i, c) for i, count in enumerate(chunk_counts) for c in range(count)]
    for q, ((i, c), keys) in enumerate(zip(places, work, strict=True)):
        rows = PAIR * chunk_counts[i]
        marks = q_refs[i][rows : rows + EXTRA, PAIR * c : PAIR * c + PAIR].astype(jnp.float32)[0:1]
        top = jnp.full((8, PAIR), LOWEST, jnp.float32)
        total = jnp.zeros((8, PAIR), jnp.float32)
        for k in keys:
            rows = key_rows[k]
            score = lax.dot_general(
                k_refs[k][0:rows, :],
                q_refs[i][PAIR * c : PAIR * c + PAIR, :],
                (((1,), (1,)), ((), ())),
                preferred_element_type=jnp.float32,
            )
            column_mark = column[k, 0:rows, :]
            tops, totals = [], []
            for half in range(2):
                part = score[:, 128 * half : 128 * half + 128]
                same = column_mark == marks[:, 128 * half : 128 * half + 128]
                if own and q == 0 and k == 0 and half == 0:
                    row = lax.broadcasted_iota(jnp.int32, (rows, 128), 0)
                    lane = lax.broadcasted_iota(jnp.int32, (rows, 128), 1)
                    same = same & (row != lane)
                part = jnp.where(same, part, LOWEST)
                weight = jnp.exp2(part * (SCALE * LOG2E) - OFFSET * LOG2E)
                tops.append(jnp.max(part.reshape(rows // 8, 8, 128), 0))
                totals.append(jnp.sum(weight.reshape(rows // 8, 8, 128), 0))
            top = jnp.maximum(top, jnp.concatenate(tops, 1))
            total = total + jnp.concatenate(totals, 1)
        out_ref[q, 0:8] = top
        out_ref[q, 8:16] = total


def stage(queries, keys, work, own, name, cost=0):
    n_key = len(keys)
    key_rows = tuple(k.shape[0] - EXTRA for k in keys)
    chunk_counts = tuple((q.shape[0] - EXTRA) // PAIR for q in queries)
    return pl.pallas_call(
        functools.partial(stage_kernel, key_rows, chunk_counts, work, own),
        out_shape=f32(sum(chunk_counts), 16, PAIR),
        in_specs=[VM] * (len(queries) + n_key),
        out_specs=VM,
        scratch_shapes=[pltpu.VMEM((n_key, PAIR, 128), jnp.float32)],
        compiler_params=pltpu.CompilerParams(vmem_limit_bytes=8 << 20),
        cost_estimate=pl.CostEstimate(flops=cost, bytes_accessed=0, transcendentals=0),
        name=name,
    )(*queries, *keys)


def collect_kernel(plan, steps, *refs):
    out_ref = refs[-1]
    straight = lax.axis_index("c") == 0
    x, y = lax.axis_index("x"), lax.axis_index("y")
    for chunk, sources in enumerate(plan):
        top = functools.reduce(jnp.maximum, [refs[s][i, 0:8] for s, i in sources])
        total = functools.reduce(jnp.add, [refs[s][i, 8:16] for s, i in sources])
        top = jnp.max(top, 0, keepdims=True)
        total = jnp.sum(total, 0, keepdims=True)
        for half in range(2):
            first, second = steps[2 * chunk + half]
            to_x = lax.rem(x + jnp.where(straight, first, second) + NX, NX)
            to_y = lax.rem(y + jnp.where(straight, second, first) + NY, NY)
            place = (to_x * NY + to_y) * 2
            out_ref[pl.ds(place, 1), :] = top[:, 128 * half : 128 * half + 128]
            out_ref[pl.ds(place + 1, 1), :] = total[:, 128 * half : 128 * half + 128]


def collect(plan, steps, stages):
    return pl.pallas_call(
        functools.partial(collect_kernel, plan, steps),
        out_shape=f32(2 * NX * NY, 128),
        in_specs=[VM] * len(stages),
        out_specs=VM,
        compiler_params=SMALL,
        name="collect",
    )(*stages)


def finish_kernel(parts_ref, top_ref, soft_ref):
    top = parts_ref[0:1, :]
    total = parts_ref[1:2, :]
    for i in range(1, NX * NY):
        top = jnp.maximum(top, parts_ref[2 * i : 2 * i + 1, :])
        total = total + parts_ref[2 * i + 1 : 2 * i + 2, :]
    top_ref[...] = top * SCALE
    soft_ref[...] = jnp.log1p(total)


def finish(parts):
    return pl.pallas_call(
        finish_kernel,
        out_shape=(f32(1, ROWS), f32(1, ROWS)),
        in_specs=[VM],
        out_specs=(VM, VM),
        compiler_params=SMALL,
        name="finish",
    )(parts)


def per_device(rows, mark):
    together = lax.optimization_barrier
    mine = prepare(rows, mark)
    a = first_axis(mine, 1)
    b = first_axis(mine, -1)
    other = swap(mine)
    z0 = pack(pack_keys_kernel, "pack_keys", PAIR, mine, other)
    t1 = away(z0)
    d = first_axis(mine, 2)
    t1, a, b, d = together((t1, a, b, d))

    t2 = away(t1)
    x = pack(pack_queries_kernel, "pack_line", 2 * PAIR, mine, a, b, d)
    e = second_axis(x, 1)
    f = second_axis(x, -1)
    s1 = stage([x], [z0, t1], ((0, 1),) * 2, True, "stage_1")
    t2, s1 = together((t2, s1))

    t3 = away(t2)
    u1 = swap(t1)
    u2 = swap(t2)
    s2 = stage([x], [t2], ((0,),) * 2, False, "stage_2")
    e, f, u1, u2, s2 = together((e, f, u1, u2, s2))

    g1 = second_axis(pack(functools.partial(half_queries_kernel, 0), "half_near", PAIR, e), 1)
    g2 = second_axis(pack(functools.partial(half_queries_kernel, 1), "half_far", PAIR, f), -1)
    s3 = stage(
        [x, e, f], [u1, u2, z0, t1, t2], ((0, 1),) * 2 + ((0, 1, 2, 3, 4),) * 4, False, "stage_3"
    )
    t4 = away(t3)
    u3 = swap(t3)
    s4 = stage([x, e, f], [t3], ((0,),) * 6, False, "stage_4")
    g1, g2, u3, s3, s4 = together((g1, g2, u3, s3, s4))

    s5 = stage(
        [x, e, f, g1, g2],
        [u3, z0, t1, u1, t2, u2, t3],
        ((0,),) * 6 + ((0, 1, 2, 3, 4, 5, 6),) * 2,
        False,
        "stage_5",
    )
    t4, s5 = together((t4, s5))
    s6 = stage([x, e, f, g1, g2], [t4], ((0,),) * 8, False, "stage_6")

    near, far = ((0, 0), (-1, 0)), ((1, 0), (-2, 0))
    move = lambda pair, step: tuple((p, step) for p, _ in pair)
    chunks = [near, far, move(near, -1), move(far, -1), move(near, 1), move(far, 1), move(near, -2), move(far, 2)]
    steps = [s for pair in chunks for s in pair]
    stages = [s1, s2, s3, s4, s5, s6]
    plan = [[(i, q) for i, s in enumerate(stages) if q < s.shape[0]] for q in range(8)]

    parts = collect(plan, steps, stages)
    parts = lax.all_to_all(parts, ("x", "y"), split_axis=0, concat_axis=0, tiled=True)
    top, soft = finish(parts)
    return top.reshape(ROWS), soft.reshape(ROWS)


def solution(mesh):
    fine = Mesh(mesh.devices.reshape(NX, NZ, NY, NC), AXES)
    return jax.shard_map(
        per_device,
        mesh=fine,
        in_specs=(P(AXES, None), P(AXES, None)),
        out_specs=(P(AXES), P(AXES)),
        check_vma=False,
    )
```

```python
import functools
import math

import jax
import jax.numpy as jnp
from jax import lax
from jax.experimental import pallas as pl
from jax.experimental.pallas import tpu as pltpu
from jax.sharding import Mesh, PartitionSpec as P

NX, NZ, NY, NC = 4, 8, 4, 2
AXES = ("x", "z", "y", "c")
ROWS = 128
WIDTH = 1024
PAIR = 2 * ROWS
EXTRA = 16
SLOT = ROWS + EXTRA
CHUNK = PAIR + EXTRA
LOWEST = -1e30
SCALE = 1.0 / math.sqrt(WIDTH)
LOG2E = math.log2(math.e)
OFFSET = 3.0
VM = pl.BlockSpec(memory_space=pltpu.VMEM)
SMALL = pltpu.CompilerParams(vmem_limit_bytes=4 << 20)


def device_index(x, z, y, c):
    return (((x % NX) * NZ + z % NZ) * NY + y % NY) * NC + c


def shift(value, move):
    pairs = []
    for x in range(NX):
        for z in range(NZ):
            for y in range(NY):
                for c in range(NC):
                    dx, dz, dy, dc = move(c)
                    target = device_index(x + dx, z + dz, y + dy, (c + dc) % NC)
                    pairs.append((device_index(x, z, y, c), target))
    return lax.ppermute(value, AXES, pairs)


def swap(value):
    return shift(value, lambda c: (0, 0, 0, 1))


def along_z(value, step):
    return shift(value, lambda c: (0, step, 0, 0))


def away(value, step=1):
    return shift(value, lambda c: (0, step, 0, 0) if c == 0 else (0, -step, 0, 0))


def first_axis(value, step):
    return shift(value, lambda c: (step, 0, 0, 0) if c == 0 else (0, 0, step, 0))


def second_axis(value, step):
    return shift(value, lambda c: (0, 0, step, 0) if c == 0 else (step, 0, 0, 0))


def bf16(*shape):
    return jax.ShapeDtypeStruct(shape, jnp.bfloat16)


def f32(*shape):
    return jax.ShapeDtypeStruct(shape, jnp.float32)


def prepare_kernel(rows_ref, mark_ref, out_ref, sem):
    copy = pltpu.make_async_copy(rows_ref, out_ref.at[pl.ds(0, ROWS)], sem)
    copy.start()
    along = jnp.broadcast_to(mark_ref[...].astype(jnp.float32), (ROWS, 128))
    wide = along.T
    lane = lax.broadcasted_iota(jnp.int32, (16, 128), 1)
    for g in range(0, 8, 2):
        both = jnp.where(lane < 64, wide[16 * g : 16 * g + 16], wide[16 * g + 16 : 16 * g + 32])
        out_ref[ROWS:SLOT, 64 * g : 64 * g + 128] = both.astype(jnp.bfloat16)
    out_ref[ROWS:SLOT, 512:640] = along[0:16].astype(jnp.bfloat16)
    out_ref[ROWS:SLOT, 640:] = jnp.zeros((16, WIDTH - 640), jnp.bfloat16)
    copy.wait()


def prepare(rows, mark):
    return pl.pallas_call(
        prepare_kernel,
        out_shape=bf16(SLOT, WIDTH),
        in_specs=[pl.BlockSpec(memory_space=pl.ANY), VM],
        out_specs=VM,
        scratch_shapes=[pltpu.SemaphoreType.DMA],
        compiler_params=SMALL,
        name="prepare",
    )(rows, mark.reshape(1, ROWS))


def pack_keys_kernel(a_ref, b_ref, out_ref):
    out_ref[0:ROWS] = a_ref[0:ROWS]
    out_ref[ROWS:PAIR] = b_ref[0:ROWS]
    out_ref[PAIR:, 0:512] = a_ref[ROWS:, 0:512]
    out_ref[PAIR:, 512:] = b_ref[ROWS:, 0:512]


def first_half_kernel(keys_ref, out_ref):
    out_ref[0:ROWS] = keys_ref[0:ROWS]
    out_ref[ROWS:] = keys_ref[PAIR:]


def pack_queries_kernel(*refs):
    out_ref = refs[-1]
    last = ROWS * (len(refs) - 1)
    for i, ref in enumerate(refs[:-1]):
        out_ref[ROWS * i : ROWS * (i + 1)] = ref[0:ROWS]
        out_ref[last:, 128 * i : 128 * i + 128] = ref[ROWS:, 512:640]
    out_ref[last:, last:] = jnp.zeros((EXTRA, WIDTH - last), jnp.bfloat16)


def half_queries_kernel(half, whole_ref, out_ref):
    out_ref[0:PAIR] = whole_ref[PAIR * half : PAIR * half + PAIR]
    out_ref[PAIR:, 0:PAIR] = whole_ref[2 * PAIR :, PAIR * half : PAIR * half + PAIR]
    out_ref[PAIR:, PAIR:] = jnp.zeros((EXTRA, WIDTH - PAIR), jnp.bfloat16)


def pack(kernel, name, rows, *parts):
    return pl.pallas_call(
        kernel,
        out_shape=bf16(rows + EXTRA, WIDTH),
        in_specs=[VM] * len(parts),
        out_specs=VM,
        compiler_params=SMALL,
        name=name,
    )(*parts)


def stage_kernel(key_rows, chunk_counts, work, own, *refs):
    n_key, n_query = len(key_rows), len(chunk_counts)
    q_refs, k_refs = refs[:n_query], refs[n_query : n_query + n_key]
    out_ref, column = refs[n_query + n_key :]

    for i, rows in enumerate(key_rows):
        for g in range(rows // 16):
            lane = 64 * g
            values = k_refs[i][rows : rows + EXTRA, lane : lane + 1].astype(jnp.float32)
            column[i, 16 * g : 16 * g + 16, :] = jnp.broadcast_to(values, (16, 128))

    places = [(i, c) for i, count in enumerate(chunk_counts) for c in range(count)]
    for q, ((i, c), keys) in enumerate(zip(places, work, strict=True)):
        rows = PAIR * chunk_counts[i]
        marks = q_refs[i][rows : rows + EXTRA, PAIR * c : PAIR * c + PAIR].astype(jnp.float32)[0:1]
        top = jnp.full((8, PAIR), LOWEST, jnp.float32)
        total = jnp.zeros((8, PAIR), jnp.float32)
        for k in keys:
            rows = key_rows[k]
            score = lax.dot_general(
                k_refs[k][0:rows, :],
                q_refs[i][PAIR * c : PAIR * c + PAIR, :],
                (((1,), (1,)), ((), ())),
                preferred_element_type=jnp.float32,
            )
            column_mark = column[k, 0:rows, :]
            tops, totals = [], []
            for half in range(2):
                part = score[:, 128 * half : 128 * half + 128]
                same = column_mark == marks[:, 128 * half : 128 * half + 128]
                if own and q == 0 and k == 0 and half == 0:
                    row = lax.broadcasted_iota(jnp.int32, (rows, 128), 0)
                    lane = lax.broadcasted_iota(jnp.int32, (rows, 128), 1)
                    same = same & (row != lane)
                power = part * (SCALE * LOG2E) + jnp.where(same, -OFFSET * LOG2E, LOWEST)
                tops.append(jnp.max(power.reshape(rows // 8, 8, 128), 0))
                totals.append(jnp.sum(jnp.exp2(power).reshape(rows // 8, 8, 128), 0))
            top = jnp.maximum(top, jnp.concatenate(tops, 1))
            total = total + jnp.concatenate(totals, 1)
        out_ref[q, 0:8] = top
        out_ref[q, 8:16] = total


def stage(queries, keys, work, own, name, cost=0):
    n_key = len(keys)
    key_rows = tuple(k.shape[0] - EXTRA for k in keys)
    chunk_counts = tuple((q.shape[0] - EXTRA) // PAIR for q in queries)
    return pl.pallas_call(
        functools.partial(stage_kernel, key_rows, chunk_counts, work, own),
        out_shape=f32(sum(chunk_counts), 16, PAIR),
        in_specs=[VM] * (len(queries) + n_key),
        out_specs=VM,
        scratch_shapes=[pltpu.VMEM((n_key, PAIR, 128), jnp.float32)],
        compiler_params=pltpu.CompilerParams(vmem_limit_bytes=8 << 20),
        cost_estimate=pl.CostEstimate(flops=cost, bytes_accessed=0, transcendentals=0),
        name=name,
    )(*queries, *keys)


def collect_kernel(plan, steps, *refs):
    out_ref = refs[-1]
    straight = lax.axis_index("c") == 0
    x, y = lax.axis_index("x"), lax.axis_index("y")
    for chunk, sources in enumerate(plan):
        top = functools.reduce(jnp.maximum, [refs[s][i, 0:8] for s, i in sources])
        total = functools.reduce(jnp.add, [refs[s][i, 8:16] for s, i in sources])
        top = jnp.max(top, 0, keepdims=True)
        total = jnp.sum(total, 0, keepdims=True)
        for half in range(2):
            first, second = steps[2 * chunk + half]
            to_x = lax.rem(x + jnp.where(straight, first, second) + NX, NX)
            to_y = lax.rem(y + jnp.where(straight, second, first) + NY, NY)
            place = (to_x * NY + to_y) * 2
            out_ref[pl.ds(place, 1), :] = top[:, 128 * half : 128 * half + 128]
            out_ref[pl.ds(place + 1, 1), :] = total[:, 128 * half : 128 * half + 128]


def collect(plan, steps, stages):
    return pl.pallas_call(
        functools.partial(collect_kernel, plan, steps),
        out_shape=f32(2 * NX * NY, 128),
        in_specs=[VM] * len(stages),
        out_specs=VM,
        compiler_params=SMALL,
        name="collect",
    )(*stages)


def finish_kernel(parts_ref, top_ref, soft_ref):
    top = parts_ref[0:1, :]
    total = parts_ref[1:2, :]
    for i in range(1, NX * NY):
        top = jnp.maximum(top, parts_ref[2 * i : 2 * i + 1, :])
        total = total + parts_ref[2 * i + 1 : 2 * i + 2, :]
    top_ref[...] = (top + OFFSET * LOG2E) * (1.0 / LOG2E)
    soft_ref[...] = jnp.log1p(total)


def finish(parts):
    return pl.pallas_call(
        finish_kernel,
        out_shape=(f32(1, ROWS), f32(1, ROWS)),
        in_specs=[VM],
        out_specs=(VM, VM),
        compiler_params=SMALL,
        name="finish",
    )(parts)


def per_device(rows, mark):
    together = lax.optimization_barrier
    mine = prepare(rows, mark)
    keys = lambda first, second: pack(pack_keys_kernel, "pack_keys", PAIR, first, second)
    a = first_axis(mine, 1)
    b = first_axis(mine, -1)
    d = first_axis(mine, 2)
    other = swap(mine)
    z0 = keys(mine, other)
    t1 = away(z0)
    x = pack(pack_queries_kernel, "pack_line", 2 * PAIR, mine, a, b, d)
    e = second_axis(x, 1)
    f = second_axis(x, -1)
    t2 = away(t1)
    s1 = stage([x], [z0, t1], ((0, 1),) * 2, True, "stage_1", 0)
    t2, s1 = together((t2, s1))

    t3 = away(t2)
    u1 = swap(t1)
    u2 = swap(t2)
    s2 = stage([x], [t2, u1, u2], ((0, 1, 2),) * 2, False, "stage_2", 0)
    e, f, s2 = together((e, f, s2))

    g1 = second_axis(pack(functools.partial(half_queries_kernel, 0), "half_near", PAIR, e), 1)
    g2 = second_axis(pack(functools.partial(half_queries_kernel, 1), "half_far", PAIR, f), -1)
    s3 = stage([e], [z0, t1, u1, t2, u2], ((0, 1, 2, 3, 4),) * 2, False, "stage_3", 0)
    t3, s3 = together((t3, s3))

    t4 = away(pack(first_half_kernel, "first_half", ROWS, t3))
    s4 = stage([f], [z0, t1, u1, t2, u2], ((0, 1, 2, 3, 4),) * 2, False, "stage_4", 0)
    t3, s4 = together((t3, s4))
    u3 = swap(t3)
    s4b = stage([x, e, f], [t3], ((0,),) * 6, False, "stage_4b")
    g1, g2, s4, s4b = together((g1, g2, s4, s4b))
    s5 = stage([g1, g2], [z0, t1, u1, t2, u2, t3], ((0, 1, 2, 3, 4, 5),) * 2, False, "stage_5", 0)
    t4, s5 = together((t4, s5))
    queries = [x, e, f, g1, g2]
    u4 = swap(t4)
    s6 = stage(queries, [u3], ((0,),) * 8, False, "stage_6")
    s7 = stage(queries, [keys(t4, u4)], ((0,),) * 8, False, "stage_7")

    near, far = ((0, 0), (-1, 0)), ((1, 0), (-2, 0))
    move = lambda pair, step: tuple((p, step) for p, _ in pair)
    chunks = [near, far, move(near, -1), move(far, -1), move(near, 1), move(far, 1), move(near, -2), move(far, 2)]
    steps = [s for pair in chunks for s in pair]
    stages = [s1, s2, s3, s4, s4b, s5, s6, s7]
    held = [(0, 1), (0, 1), (2, 3), (4, 5), range(6), (6, 7), range(8), range(8)]
    plan = [[(i, list(h).index(q)) for i, h in enumerate(held) if q in h] for q in range(8)]

    parts = collect(plan, steps, stages)
    parts = lax.all_to_all(parts, ("x", "y"), split_axis=0, concat_axis=0, tiled=True)
    top, soft = finish(parts)
    return top.reshape(ROWS), soft.reshape(ROWS)


def solution(mesh):
    fine = Mesh(mesh.devices.reshape(NX, NZ, NY, NC), AXES)
    return jax.shard_map(
        per_device,
        mesh=fine,
        in_specs=(P(AXES, None), P(AXES, None)),
        out_specs=(P(AXES), P(AXES)),
        check_vma=False,
    )
```

```python
import functools
import math

import jax
import jax.numpy as jnp
from jax import lax
from jax.experimental import pallas as pl
from jax.experimental.pallas import tpu as pltpu
from jax.sharding import Mesh, PartitionSpec as P

NX, NZ, NY, NC = 4, 8, 4, 2
AXES = ("x", "z", "y", "c")
ROWS = 128
WIDTH = 1024
PAIR = 2 * ROWS
EXTRA = 16
SLOT = ROWS + EXTRA
CHUNK = PAIR + EXTRA
LOWEST = -1e30
SCALE = 1.0 / math.sqrt(WIDTH)
LOG2E = math.log2(math.e)
OFFSET = 3.0
VM = pl.BlockSpec(memory_space=pltpu.VMEM)
SMALL = pltpu.CompilerParams(vmem_limit_bytes=4 << 20)


def device_index(x, z, y, c):
    return (((x % NX) * NZ + z % NZ) * NY + y % NY) * NC + c


def shift(value, move):
    pairs = []
    for x in range(NX):
        for z in range(NZ):
            for y in range(NY):
                for c in range(NC):
                    dx, dz, dy, dc = move(c)
                    target = device_index(x + dx, z + dz, y + dy, (c + dc) % NC)
                    pairs.append((device_index(x, z, y, c), target))
    return lax.ppermute(value, AXES, pairs)


def swap(value):
    return shift(value, lambda c: (0, 0, 0, 1))


def along_z(value, step):
    return shift(value, lambda c: (0, step, 0, 0))


def away(value, step=1):
    return shift(value, lambda c: (0, step, 0, 0) if c == 0 else (0, -step, 0, 0))


def first_axis(value, step):
    return shift(value, lambda c: (step, 0, 0, 0) if c == 0 else (0, 0, step, 0))


def second_axis(value, step):
    return shift(value, lambda c: (0, 0, step, 0) if c == 0 else (step, 0, 0, 0))


def bf16(*shape):
    return jax.ShapeDtypeStruct(shape, jnp.bfloat16)


def f32(*shape):
    return jax.ShapeDtypeStruct(shape, jnp.float32)


def prepare_kernel(rows_ref, mark_ref, out_ref, sem):
    copy = pltpu.make_async_copy(rows_ref, out_ref.at[pl.ds(0, ROWS)], sem)
    copy.start()
    along = jnp.broadcast_to(mark_ref[...].astype(jnp.float32), (ROWS, 128))
    wide = along.T
    lane = lax.broadcasted_iota(jnp.int32, (16, 128), 1)
    for g in range(0, 8, 2):
        both = jnp.where(lane < 64, wide[16 * g : 16 * g + 16], wide[16 * g + 16 : 16 * g + 32])
        out_ref[ROWS:SLOT, 64 * g : 64 * g + 128] = both.astype(jnp.bfloat16)
    out_ref[ROWS:SLOT, 512:640] = along[0:16].astype(jnp.bfloat16)
    out_ref[ROWS:SLOT, 640:] = jnp.zeros((16, WIDTH - 640), jnp.bfloat16)
    copy.wait()


def prepare(rows, mark):
    return pl.pallas_call(
        prepare_kernel,
        out_shape=bf16(SLOT, WIDTH),
        in_specs=[pl.BlockSpec(memory_space=pl.ANY), VM],
        out_specs=VM,
        scratch_shapes=[pltpu.SemaphoreType.DMA],
        compiler_params=SMALL,
        name="prepare",
    )(rows, mark.reshape(1, ROWS))


def pack_keys_kernel(a_ref, b_ref, out_ref):
    out_ref[0:ROWS] = a_ref[0:ROWS]
    out_ref[ROWS:PAIR] = b_ref[0:ROWS]
    out_ref[PAIR:, 0:512] = a_ref[ROWS:, 0:512]
    out_ref[PAIR:, 512:] = b_ref[ROWS:, 0:512]


def first_half_kernel(keys_ref, out_ref):
    out_ref[0:ROWS] = keys_ref[0:ROWS]
    out_ref[ROWS:] = keys_ref[PAIR:]


def pack_queries_kernel(*refs):
    out_ref = refs[-1]
    last = ROWS * (len(refs) - 1)
    for i, ref in enumerate(refs[:-1]):
        out_ref[ROWS * i : ROWS * (i + 1)] = ref[0:ROWS]
        out_ref[last:, 128 * i : 128 * i + 128] = ref[ROWS:, 512:640]
    out_ref[last:, last:] = jnp.zeros((EXTRA, WIDTH - last), jnp.bfloat16)


def half_queries_kernel(half, whole_ref, out_ref):
    out_ref[0:PAIR] = whole_ref[PAIR * half : PAIR * half + PAIR]
    out_ref[PAIR:, 0:PAIR] = whole_ref[2 * PAIR :, PAIR * half : PAIR * half + PAIR]
    out_ref[PAIR:, PAIR:] = jnp.zeros((EXTRA, WIDTH - PAIR), jnp.bfloat16)


def pack(kernel, name, rows, *parts):
    return pl.pallas_call(
        kernel,
        out_shape=bf16(rows + EXTRA, WIDTH),
        in_specs=[VM] * len(parts),
        out_specs=VM,
        compiler_params=SMALL,
        name=name,
    )(*parts)


def stage_kernel(key_rows, chunk_counts, work, own, *refs):
    n_key, n_query = len(key_rows), len(chunk_counts)
    q_refs, k_refs = refs[:n_query], refs[n_query : n_query + n_key]
    out_ref, column = refs[n_query + n_key :]

    for i, rows in enumerate(key_rows):
        for g in range(rows // 16):
            lane = 64 * g
            values = k_refs[i][rows : rows + EXTRA, lane : lane + 1].astype(jnp.float32)
            column[i, 16 * g : 16 * g + 16, :] = jnp.broadcast_to(values, (16, 128))

    places = [(i, c) for i, count in enumerate(chunk_counts) for c in range(count)]
    for q, ((i, c), keys) in enumerate(zip(places, work, strict=True)):
        rows = PAIR * chunk_counts[i]
        marks = q_refs[i][rows : rows + EXTRA, PAIR * c : PAIR * c + PAIR].astype(jnp.float32)[0:1]
        top = jnp.full((8, PAIR), LOWEST, jnp.float32)
        total = jnp.zeros((8, PAIR), jnp.float32)
        for k in keys:
            rows = key_rows[k]
            score = lax.dot_general(
                k_refs[k][0:rows, :],
                q_refs[i][PAIR * c : PAIR * c + PAIR, :],
                (((1,), (1,)), ((), ())),
                preferred_element_type=jnp.float32,
            )
            column_mark = column[k, 0:rows, :]
            tops, totals = [], []
            for half in range(2):
                part = score[:, 128 * half : 128 * half + 128]
                same = column_mark == marks[:, 128 * half : 128 * half + 128]
                if own and q == 0 and k == 0 and half == 0:
                    row = lax.broadcasted_iota(jnp.int32, (rows, 128), 0)
                    lane = lax.broadcasted_iota(jnp.int32, (rows, 128), 1)
                    same = same & (row != lane)
                power = part * (SCALE * LOG2E) + jnp.where(same, -OFFSET * LOG2E, LOWEST)
                tops.append(jnp.max(power.reshape(rows // 8, 8, 128), 0))
                totals.append(jnp.sum(jnp.exp2(power).reshape(rows // 8, 8, 128), 0))
            top = jnp.maximum(top, jnp.concatenate(tops, 1))
            total = total + jnp.concatenate(totals, 1)
        out_ref[q, 0:8] = top
        out_ref[q, 8:16] = total


def stage(queries, keys, work, own, name, cost=0):
    n_key = len(keys)
    key_rows = tuple(k.shape[0] - EXTRA for k in keys)
    chunk_counts = tuple((q.shape[0] - EXTRA) // PAIR for q in queries)
    return pl.pallas_call(
        functools.partial(stage_kernel, key_rows, chunk_counts, work, own),
        out_shape=f32(sum(chunk_counts), 16, PAIR),
        in_specs=[VM] * (len(queries) + n_key),
        out_specs=VM,
        scratch_shapes=[pltpu.VMEM((n_key, PAIR, 128), jnp.float32)],
        compiler_params=pltpu.CompilerParams(vmem_limit_bytes=8 << 20),
        cost_estimate=pl.CostEstimate(flops=cost, bytes_accessed=0, transcendentals=0),
        name=name,
    )(*queries, *keys)


def collect_kernel(plan, steps, *refs):
    out_ref = refs[-1]
    straight = lax.axis_index("c") == 0
    x, y = lax.axis_index("x"), lax.axis_index("y")
    for chunk, sources in enumerate(plan):
        top = functools.reduce(jnp.maximum, [refs[s][i, 0:8] for s, i in sources])
        total = functools.reduce(jnp.add, [refs[s][i, 8:16] for s, i in sources])
        top = jnp.max(top, 0, keepdims=True)
        total = jnp.sum(total, 0, keepdims=True)
        for half in range(2):
            first, second = steps[2 * chunk + half]
            to_x = lax.rem(x + jnp.where(straight, first, second) + NX, NX)
            to_y = lax.rem(y + jnp.where(straight, second, first) + NY, NY)
            place = (to_x * NY + to_y) * 2
            out_ref[pl.ds(place, 1), :] = top[:, 128 * half : 128 * half + 128]
            out_ref[pl.ds(place + 1, 1), :] = total[:, 128 * half : 128 * half + 128]


def collect(plan, steps, stages):
    return pl.pallas_call(
        functools.partial(collect_kernel, plan, steps),
        out_shape=f32(2 * NX * NY, 128),
        in_specs=[VM] * len(stages),
        out_specs=VM,
        compiler_params=SMALL,
        name="collect",
    )(*stages)


def finish_kernel(parts_ref, top_ref, soft_ref):
    top = parts_ref[0:1, :]
    total = parts_ref[1:2, :]
    for i in range(1, NX * NY):
        top = jnp.maximum(top, parts_ref[2 * i : 2 * i + 1, :])
        total = total + parts_ref[2 * i + 1 : 2 * i + 2, :]
    top_ref[...] = (top + OFFSET * LOG2E) * (1.0 / LOG2E)
    soft_ref[...] = jnp.log1p(total)


def finish(parts):
    return pl.pallas_call(
        finish_kernel,
        out_shape=(f32(1, ROWS), f32(1, ROWS)),
        in_specs=[VM],
        out_specs=(VM, VM),
        compiler_params=SMALL,
        name="finish",
    )(parts)


def per_device(rows, mark):
    together = lax.optimization_barrier
    mine = prepare(rows, mark)
    keys = lambda first, second: pack(pack_keys_kernel, "pack_keys", PAIR, first, second)
    a = first_axis(mine, 1)
    b = first_axis(mine, -1)
    d = first_axis(mine, 2)
    other = swap(mine)
    z0 = keys(mine, other)
    t1 = away(z0)
    x = pack(pack_queries_kernel, "pack_line", 2 * PAIR, mine, d, a, b)
    e = second_axis(x, 1)
    f = second_axis(x, -1)
    t2 = away(t1)
    s1 = stage([x], [z0, t1], ((0, 1),) * 2, True, "stage_1", 0)
    t2, s1 = together((t2, s1))

    t3 = away(t2)
    u1 = swap(t1)
    u2 = swap(t2)
    s2 = stage([x], [t2, u1, u2], ((0, 1, 2),) * 2, False, "stage_2", 0)
    e, f, s2 = together((e, f, s2))

    g1 = second_axis(pack(functools.partial(half_queries_kernel, 0), "half_near", PAIR, e), 1)
    g2 = second_axis(pack(functools.partial(half_queries_kernel, 1), "half_far", PAIR, f), -1)
    s3 = stage([e], [z0, t1, u1, t2, u2], ((0, 1, 2, 3, 4),) * 2, False, "stage_3", 0)
    t3, s3 = together((t3, s3))

    t4 = away(pack(first_half_kernel, "first_half", ROWS, t3))
    s4 = stage([f], [z0, t1, u1, t2, u2], ((0, 1, 2, 3, 4),) * 2, False, "stage_4", 0)
    t3, s4 = together((t3, s4))
    u3 = swap(t3)
    s4b = stage([x, e, f], [t3], ((0,),) * 6, False, "stage_4b")
    g1, g2, s4, s4b = together((g1, g2, s4, s4b))
    s5 = stage([g1, g2], [z0, t1, u1, t2, u2, t3], ((0, 1, 2, 3, 4, 5),) * 2, False, "stage_5", 0)
    t4, s5 = together((t4, s5))
    queries = [x, e, f, g1, g2]
    u4 = swap(t4)
    s6 = stage(queries, [u3], ((0,),) * 8, False, "stage_6")
    s7 = stage(queries, [keys(t4, u4)], ((0,),) * 8, False, "stage_7")

    near, far = ((0, 0), (-2, 0)), ((-1, 0), (1, 0))
    move = lambda pair, step: tuple((p, step) for p, _ in pair)
    chunks = [near, far, move(near, -1), move(far, -1), move(near, 1), move(far, 1), move(near, -2), move(far, 2)]
    steps = [s for pair in chunks for s in pair]
    stages = [s1, s2, s3, s4, s4b, s5, s6, s7]
    held = [(0, 1), (0, 1), (2, 3), (4, 5), range(6), (6, 7), range(8), range(8)]
    plan = [[(i, list(h).index(q)) for i, h in enumerate(held) if q in h] for q in range(8)]

    parts = collect(plan, steps, stages)
    parts = lax.all_to_all(parts, ("x", "y"), split_axis=0, concat_axis=0, tiled=True)
    top, soft = finish(parts)
    return top.reshape(ROWS), soft.reshape(ROWS)


def solution(mesh):
    fine = Mesh(mesh.devices.reshape(NX, NZ, NY, NC), AXES)
    return jax.shard_map(
        per_device,
        mesh=fine,
        in_specs=(P(AXES, None), P(AXES, None)),
        out_specs=(P(AXES), P(AXES)),
        check_vma=False,
    )
```

```python
import functools
import math

import jax
import jax.numpy as jnp
from jax import lax
from jax.experimental import pallas as pl
from jax.experimental.pallas import tpu as pltpu
from jax.sharding import Mesh, PartitionSpec as P

NX, NZ, NY, NC = 4, 8, 4, 2
AXES = ("x", "z", "y", "c")
ROWS = 128
WIDTH = 1024
PAIR = 2 * ROWS
EXTRA = 16
SLOT = ROWS + EXTRA
CHUNK = PAIR + EXTRA
LOWEST = -1e30
SCALE = 1.0 / math.sqrt(WIDTH)
LOG2E = math.log2(math.e)
OFFSET = 3.0
VM = pl.BlockSpec(memory_space=pltpu.VMEM)
SMALL = pltpu.CompilerParams(vmem_limit_bytes=4 << 20)


def device_index(x, z, y, c):
    return (((x % NX) * NZ + z % NZ) * NY + y % NY) * NC + c


def shift(value, move):
    pairs = []
    for x in range(NX):
        for z in range(NZ):
            for y in range(NY):
                for c in range(NC):
                    dx, dz, dy, dc = move(c)
                    target = device_index(x + dx, z + dz, y + dy, (c + dc) % NC)
                    pairs.append((device_index(x, z, y, c), target))
    return lax.ppermute(value, AXES, pairs)


def swap(value):
    return shift(value, lambda c: (0, 0, 0, 1))


def along_z(value, step):
    return shift(value, lambda c: (0, step, 0, 0))


def away(value, step=1):
    return shift(value, lambda c: (0, step, 0, 0) if c == 0 else (0, -step, 0, 0))


def first_axis(value, step):
    return shift(value, lambda c: (step, 0, 0, 0) if c == 0 else (0, 0, step, 0))


def second_axis(value, step):
    return shift(value, lambda c: (0, 0, step, 0) if c == 0 else (step, 0, 0, 0))


def bf16(*shape):
    return jax.ShapeDtypeStruct(shape, jnp.bfloat16)


def f32(*shape):
    return jax.ShapeDtypeStruct(shape, jnp.float32)


def prepare_kernel(rows_ref, mark_ref, out_ref, sem):
    copy = pltpu.make_async_copy(rows_ref, out_ref.at[pl.ds(0, ROWS)], sem)
    copy.start()
    along = jnp.broadcast_to(mark_ref[...].astype(jnp.float32), (ROWS, 128))
    wide = along.T
    lane = lax.broadcasted_iota(jnp.int32, (16, 128), 1)
    for g in range(0, 8, 2):
        both = jnp.where(lane < 64, wide[16 * g : 16 * g + 16], wide[16 * g + 16 : 16 * g + 32])
        out_ref[ROWS:SLOT, 64 * g : 64 * g + 128] = both.astype(jnp.bfloat16)
    out_ref[ROWS:SLOT, 512:640] = along[0:16].astype(jnp.bfloat16)
    out_ref[ROWS:SLOT, 640:] = jnp.zeros((16, WIDTH - 640), jnp.bfloat16)
    copy.wait()


def prepare(rows, mark):
    return pl.pallas_call(
        prepare_kernel,
        out_shape=bf16(SLOT, WIDTH),
        in_specs=[pl.BlockSpec(memory_space=pl.ANY), VM],
        out_specs=VM,
        scratch_shapes=[pltpu.SemaphoreType.DMA],
        compiler_params=SMALL,
        name="prepare",
    )(rows, mark.reshape(1, ROWS))


def pack_keys_kernel(a_ref, b_ref, out_ref):
    out_ref[0:ROWS] = a_ref[0:ROWS]
    out_ref[ROWS:PAIR] = b_ref[0:ROWS]
    out_ref[PAIR:, 0:512] = a_ref[ROWS:, 0:512]
    out_ref[PAIR:, 512:] = b_ref[ROWS:, 0:512]


def first_half_kernel(keys_ref, out_ref):
    out_ref[0:ROWS] = keys_ref[0:ROWS]
    out_ref[ROWS:] = keys_ref[PAIR:]


def pack_queries_kernel(*refs):
    out_ref = refs[-1]
    last = ROWS * (len(refs) - 1)
    for i, ref in enumerate(refs[:-1]):
        out_ref[ROWS * i : ROWS * (i + 1)] = ref[0:ROWS]
        out_ref[last:, 128 * i : 128 * i + 128] = ref[ROWS:, 512:640]
    out_ref[last:, last:] = jnp.zeros((EXTRA, WIDTH - last), jnp.bfloat16)


def half_queries_kernel(half, whole_ref, out_ref):
    out_ref[0:PAIR] = whole_ref[PAIR * half : PAIR * half + PAIR]
    out_ref[PAIR:, 0:PAIR] = whole_ref[2 * PAIR :, PAIR * half : PAIR * half + PAIR]
    out_ref[PAIR:, PAIR:] = jnp.zeros((EXTRA, WIDTH - PAIR), jnp.bfloat16)


def pack(kernel, name, rows, *parts):
    return pl.pallas_call(
        kernel,
        out_shape=bf16(rows + EXTRA, WIDTH),
        in_specs=[VM] * len(parts),
        out_specs=VM,
        compiler_params=SMALL,
        name=name,
    )(*parts)


def stage_kernel(key_rows, chunk_counts, work, own, *refs):
    n_key, n_query = len(key_rows), len(chunk_counts)
    q_refs, k_refs = refs[:n_query], refs[n_query : n_query + n_key]
    out_ref, column = refs[n_query + n_key :]

    for i, rows in enumerate(key_rows):
        for g in range(rows // 16):
            lane = 64 * g
            values = k_refs[i][rows : rows + EXTRA, lane : lane + 1].astype(jnp.float32)
            column[i, 16 * g : 16 * g + 16, :] = jnp.broadcast_to(values, (16, 128))

    places = [(i, c) for i, count in enumerate(chunk_counts) for c in range(count)]
    for q, ((i, c), keys) in enumerate(zip(places, work, strict=True)):
        rows = PAIR * chunk_counts[i]
        marks = q_refs[i][rows : rows + EXTRA, PAIR * c : PAIR * c + PAIR].astype(jnp.float32)[0:1]
        top = jnp.full((8, PAIR), LOWEST, jnp.float32)
        total = jnp.zeros((8, PAIR), jnp.float32)
        for k in keys:
            rows = key_rows[k]
            score = lax.dot_general(
                k_refs[k][0:rows, :],
                q_refs[i][PAIR * c : PAIR * c + PAIR, :],
                (((1,), (1,)), ((), ())),
                preferred_element_type=jnp.float32,
            )
            column_mark = column[k, 0:rows, :]
            tops, totals = [], []
            for half in range(2):
                part = score[:, 128 * half : 128 * half + 128]
                same = column_mark == marks[:, 128 * half : 128 * half + 128]
                if own and q == 0 and k == 0 and half == 0:
                    row = lax.broadcasted_iota(jnp.int32, (rows, 128), 0)
                    lane = lax.broadcasted_iota(jnp.int32, (rows, 128), 1)
                    same = same & (row != lane)
                power = part * (SCALE * LOG2E) + jnp.where(same, -OFFSET * LOG2E, LOWEST)
                tops.append(jnp.max(power.reshape(rows // 8, 8, 128), 0))
                totals.append(jnp.sum(jnp.exp2(power).reshape(rows // 8, 8, 128), 0))
            top = jnp.maximum(top, jnp.concatenate(tops, 1))
            total = total + jnp.concatenate(totals, 1)
        out_ref[q, 0:8] = top
        out_ref[q, 8:16] = total


def stage(queries, keys, work, own, name, cost=0):
    n_key = len(keys)
    key_rows = tuple(k.shape[0] - EXTRA for k in keys)
    chunk_counts = tuple((q.shape[0] - EXTRA) // PAIR for q in queries)
    return pl.pallas_call(
        functools.partial(stage_kernel, key_rows, chunk_counts, work, own),
        out_shape=f32(sum(chunk_counts), 16, PAIR),
        in_specs=[VM] * (len(queries) + n_key),
        out_specs=VM,
        scratch_shapes=[pltpu.VMEM((n_key, PAIR, 128), jnp.float32)],
        compiler_params=pltpu.CompilerParams(vmem_limit_bytes=8 << 20),
        cost_estimate=pl.CostEstimate(flops=cost, bytes_accessed=0, transcendentals=0),
        name=name,
    )(*queries, *keys)


def collect_kernel(plan, steps, *refs):
    out_ref = refs[-1]
    straight = lax.axis_index("c") == 0
    x, y = lax.axis_index("x"), lax.axis_index("y")
    for chunk, sources in enumerate(plan):
        top = functools.reduce(jnp.maximum, [refs[s][i, 0:8] for s, i in sources])
        total = functools.reduce(jnp.add, [refs[s][i, 8:16] for s, i in sources])
        top = jnp.max(top, 0, keepdims=True)
        total = jnp.sum(total, 0, keepdims=True)
        for half in range(2):
            first, second = steps[2 * chunk + half]
            to_x = lax.rem(x + jnp.where(straight, first, second) + NX, NX)
            to_y = lax.rem(y + jnp.where(straight, second, first) + NY, NY)
            place = (to_x * NY + to_y) * 2
            out_ref[pl.ds(place, 1), :] = top[:, 128 * half : 128 * half + 128]
            out_ref[pl.ds(place + 1, 1), :] = total[:, 128 * half : 128 * half + 128]


def collect(plan, steps, stages):
    return pl.pallas_call(
        functools.partial(collect_kernel, plan, steps),
        out_shape=f32(2 * NX * NY, 128),
        in_specs=[VM] * len(stages),
        out_specs=VM,
        compiler_params=SMALL,
        name="collect",
    )(*stages)


def finish_kernel(parts_ref, top_ref, soft_ref):
    top = parts_ref[0:1, :]
    total = parts_ref[1:2, :]
    for i in range(1, NX * NY):
        top = jnp.maximum(top, parts_ref[2 * i : 2 * i + 1, :])
        total = total + parts_ref[2 * i + 1 : 2 * i + 2, :]
    top_ref[...] = (top + OFFSET * LOG2E) * (1.0 / LOG2E)
    soft_ref[...] = jnp.log1p(total)


def finish(parts):
    return pl.pallas_call(
        finish_kernel,
        out_shape=(f32(1, ROWS), f32(1, ROWS)),
        in_specs=[VM],
        out_specs=(VM, VM),
        compiler_params=SMALL,
        name="finish",
    )(parts)


def per_device(rows, mark):
    together = lax.optimization_barrier
    mine = prepare(rows, mark)
    keys = lambda first, second: pack(pack_keys_kernel, "pack_keys", PAIR, first, second)
    a = first_axis(mine, 1)
    b = first_axis(mine, -1)
    d = first_axis(mine, 2)
    other = swap(mine)
    z0 = keys(mine, other)
    t1 = away(z0)
    x = pack(pack_queries_kernel, "pack_line", 2 * PAIR, mine, a, b, d)
    e = second_axis(x, 1)
    f = second_axis(x, -1)
    s0 = stage([x], [z0], ((0,),) * 2, True, "stage_0", 3000000000)
    t1, s0 = together((t1, s0))
    t2 = away(t1)
    u1 = swap(t1)
    s1 = stage([x], [t1], ((0,),) * 2, False, "stage_1", 10000000000)
    t2, u1, s1 = together((t2, u1, s1))

    t3 = away(t2)
    u2 = swap(t2)
    s2 = stage([x], [t2, u1, u2], ((0, 1, 2),) * 2, False, "stage_2", 0)
    e, f, s2 = together((e, f, s2))

    g1 = second_axis(pack(functools.partial(half_queries_kernel, 0), "half_near", PAIR, e), 1)
    g2 = second_axis(pack(functools.partial(half_queries_kernel, 1), "half_far", PAIR, f), -1)
    s3 = stage([e], [z0, t1, u1, t2, u2], ((0, 1, 2, 3, 4),) * 2, False, "stage_3", 0)
    t3, s3 = together((t3, s3))

    t4 = away(pack(first_half_kernel, "first_half", ROWS, t3))
    s4 = stage([f], [z0, t1, u1, t2, u2], ((0, 1, 2, 3, 4),) * 2, False, "stage_4", 0)
    t3, s4 = together((t3, s4))
    u3 = swap(t3)
    s4b = stage([x, e, f], [t3], ((0,),) * 6, False, "stage_4b")
    g1, g2, s4, s4b = together((g1, g2, s4, s4b))
    s5 = stage([g1, g2], [z0, t1, u1, t2, u2, t3], ((0, 1, 2, 3, 4, 5),) * 2, False, "stage_5", 0)
    t4, s5 = together((t4, s5))
    queries = [x, e, f, g1, g2]
    u4 = swap(t4)
    s6 = stage(queries, [u3], ((0,),) * 8, False, "stage_6")
    s7 = stage(queries, [keys(t4, u4)], ((0,),) * 8, False, "stage_7")

    near, far = ((0, 0), (-1, 0)), ((1, 0), (-2, 0))
    move = lambda pair, step: tuple((p, step) for p, _ in pair)
    chunks = [near, far, move(near, -1), move(far, -1), move(near, 1), move(far, 1), move(near, -2), move(far, 2)]
    steps = [s for pair in chunks for s in pair]
    stages = [s0, s1, s2, s3, s4, s4b, s5, s6, s7]
    held = [(0, 1), (0, 1), (0, 1), (2, 3), (4, 5), range(6), (6, 7), range(8), range(8)]
    plan = [[(i, list(h).index(q)) for i, h in enumerate(held) if q in h] for q in range(8)]

    parts = collect(plan, steps, stages)
    parts = lax.all_to_all(parts, ("x", "y"), split_axis=0, concat_axis=0, tiled=True)
    top, soft = finish(parts)
    return top.reshape(ROWS), soft.reshape(ROWS)


def solution(mesh):
    fine = Mesh(mesh.devices.reshape(NX, NZ, NY, NC), AXES)
    return jax.shard_map(
        per_device,
        mesh=fine,
        in_specs=(P(AXES, None), P(AXES, None)),
        out_specs=(P(AXES), P(AXES)),
        check_vma=False,
    )
```

```python
import functools
import math

import jax
import jax.numpy as jnp
from jax import lax
from jax.experimental import pallas as pl
from jax.experimental.pallas import tpu as pltpu
from jax.sharding import Mesh, PartitionSpec as P

NX, NZ, NY, NC = 4, 8, 4, 2
AXES = ("x", "z", "y", "c")
ROWS = 128
WIDTH = 1024
PAIR = 2 * ROWS
EXTRA = 16
SLOT = ROWS + EXTRA
CHUNK = PAIR + EXTRA
LOWEST = -1e30
SCALE = 1.0 / math.sqrt(WIDTH)
LOG2E = math.log2(math.e)
OFFSET = 3.0
VM = pl.BlockSpec(memory_space=pltpu.VMEM)
SMALL = pltpu.CompilerParams(vmem_limit_bytes=4 << 20)


def device_index(x, z, y, c):
    return (((x % NX) * NZ + z % NZ) * NY + y % NY) * NC + c


def shift(value, move):
    pairs = []
    for x in range(NX):
        for z in range(NZ):
            for y in range(NY):
                for c in range(NC):
                    dx, dz, dy, dc = move(c)
                    target = device_index(x + dx, z + dz, y + dy, (c + dc) % NC)
                    pairs.append((device_index(x, z, y, c), target))
    return lax.ppermute(value, AXES, pairs)


def swap(value):
    return shift(value, lambda c: (0, 0, 0, 1))


def along_z(value, step):
    return shift(value, lambda c: (0, step, 0, 0))


def away(value, step=1):
    return shift(value, lambda c: (0, step, 0, 0) if c == 0 else (0, -step, 0, 0))


def first_axis(value, step):
    return shift(value, lambda c: (step, 0, 0, 0) if c == 0 else (0, 0, step, 0))


def second_axis(value, step):
    return shift(value, lambda c: (0, 0, step, 0) if c == 0 else (step, 0, 0, 0))


def bf16(*shape):
    return jax.ShapeDtypeStruct(shape, jnp.bfloat16)


def f32(*shape):
    return jax.ShapeDtypeStruct(shape, jnp.float32)


def prepare_kernel(rows_ref, mark_ref, out_ref, sem):
    copy = pltpu.make_async_copy(rows_ref, out_ref.at[pl.ds(0, ROWS)], sem)
    copy.start()
    along = jnp.broadcast_to(mark_ref[...].astype(jnp.float32), (ROWS, 128))
    wide = along.T
    lane = lax.broadcasted_iota(jnp.int32, (16, 128), 1)
    for g in range(0, 8, 2):
        both = jnp.where(lane < 64, wide[16 * g : 16 * g + 16], wide[16 * g + 16 : 16 * g + 32])
        out_ref[ROWS:SLOT, 64 * g : 64 * g + 128] = both.astype(jnp.bfloat16)
    out_ref[ROWS:SLOT, 512:640] = along[0:16].astype(jnp.bfloat16)
    out_ref[ROWS:SLOT, 640:] = jnp.zeros((16, WIDTH - 640), jnp.bfloat16)
    copy.wait()


def prepare(rows, mark):
    return pl.pallas_call(
        prepare_kernel,
        out_shape=bf16(SLOT, WIDTH),
        in_specs=[pl.BlockSpec(memory_space=pl.ANY), VM],
        out_specs=VM,
        scratch_shapes=[pltpu.SemaphoreType.DMA],
        compiler_params=SMALL,
        name="prepare",
    )(rows, mark.reshape(1, ROWS))


def pack_keys_kernel(a_ref, b_ref, out_ref):
    out_ref[0:ROWS] = a_ref[0:ROWS]
    out_ref[ROWS:PAIR] = b_ref[0:ROWS]
    out_ref[PAIR:, 0:512] = a_ref[ROWS:, 0:512]
    out_ref[PAIR:, 512:] = b_ref[ROWS:, 0:512]


def first_half_kernel(keys_ref, out_ref):
    out_ref[0:ROWS] = keys_ref[0:ROWS]
    out_ref[ROWS:] = keys_ref[PAIR:]


def pack_queries_kernel(*refs):
    out_ref = refs[-1]
    last = ROWS * (len(refs) - 1)
    for i, ref in enumerate(refs[:-1]):
        out_ref[ROWS * i : ROWS * (i + 1)] = ref[0:ROWS]
        out_ref[last:, 128 * i : 128 * i + 128] = ref[ROWS:, 512:640]
    out_ref[last:, last:] = jnp.zeros((EXTRA, WIDTH - last), jnp.bfloat16)


def half_queries_kernel(half, whole_ref, out_ref):
    out_ref[0:PAIR] = whole_ref[PAIR * half : PAIR * half + PAIR]
    out_ref[PAIR:, 0:PAIR] = whole_ref[2 * PAIR :, PAIR * half : PAIR * half + PAIR]
    out_ref[PAIR:, PAIR:] = jnp.zeros((EXTRA, WIDTH - PAIR), jnp.bfloat16)


def pack(kernel, name, rows, *parts):
    return pl.pallas_call(
        kernel,
        out_shape=bf16(rows + EXTRA, WIDTH),
        in_specs=[VM] * len(parts),
        out_specs=VM,
        compiler_params=SMALL,
        name=name,
    )(*parts)


def stage_kernel(key_rows, chunk_counts, work, own, *refs):
    n_key, n_query = len(key_rows), len(chunk_counts)
    q_refs, k_refs = refs[:n_query], refs[n_query : n_query + n_key]
    out_ref, column = refs[n_query + n_key :]

    for i, rows in enumerate(key_rows):
        for g in range(rows // 16):
            lane = 64 * g
            values = k_refs[i][rows : rows + EXTRA, lane : lane + 1].astype(jnp.float32)
            column[i, 16 * g : 16 * g + 16, :] = jnp.broadcast_to(values, (16, 128))

    places = [(i, c) for i, count in enumerate(chunk_counts) for c in range(count)]
    for q, ((i, c), keys) in enumerate(zip(places, work, strict=True)):
        rows = PAIR * chunk_counts[i]
        marks = q_refs[i][rows : rows + EXTRA, PAIR * c : PAIR * c + PAIR].astype(jnp.float32)[0:1]
        top = jnp.full((8, PAIR), LOWEST, jnp.float32)
        total = jnp.zeros((8, PAIR), jnp.float32)
        for k in keys:
            rows = key_rows[k]
            score = lax.dot_general(
                k_refs[k][0:rows, :],
                q_refs[i][PAIR * c : PAIR * c + PAIR, :],
                (((1,), (1,)), ((), ())),
                preferred_element_type=jnp.float32,
            )
            column_mark = column[k, 0:rows, :]
            tops, totals = [], []
            for half in range(2):
                part = score[:, 128 * half : 128 * half + 128]
                same = column_mark == marks[:, 128 * half : 128 * half + 128]
                if own and q == 0 and k == 0 and half == 0:
                    row = lax.broadcasted_iota(jnp.int32, (rows, 128), 0)
                    lane = lax.broadcasted_iota(jnp.int32, (rows, 128), 1)
                    same = same & (row != lane)
                power = part * (SCALE * LOG2E) + jnp.where(same, -OFFSET * LOG2E, LOWEST)
                tops.append(jnp.max(power.reshape(rows // 8, 8, 128), 0))
                totals.append(jnp.sum(jnp.exp2(power).reshape(rows // 8, 8, 128), 0))
            top = jnp.maximum(top, jnp.concatenate(tops, 1))
            total = total + jnp.concatenate(totals, 1)
        out_ref[q, 0:8] = top
        out_ref[q, 8:16] = total


def stage(queries, keys, work, own, name, cost=0):
    n_key = len(keys)
    key_rows = tuple(k.shape[0] - EXTRA for k in keys)
    chunk_counts = tuple((q.shape[0] - EXTRA) // PAIR for q in queries)
    return pl.pallas_call(
        functools.partial(stage_kernel, key_rows, chunk_counts, work, own),
        out_shape=f32(sum(chunk_counts), 16, PAIR),
        in_specs=[VM] * (len(queries) + n_key),
        out_specs=VM,
        scratch_shapes=[pltpu.VMEM((n_key, PAIR, 128), jnp.float32)],
        compiler_params=pltpu.CompilerParams(vmem_limit_bytes=8 << 20),
        cost_estimate=pl.CostEstimate(flops=cost, bytes_accessed=0, transcendentals=0),
        name=name,
    )(*queries, *keys)


def collect_kernel(plan, steps, *refs):
    out_ref = refs[-1]
    straight = lax.axis_index("c") == 0
    x, y = lax.axis_index("x"), lax.axis_index("y")
    for chunk, sources in enumerate(plan):
        top = functools.reduce(jnp.maximum, [refs[s][i, 0:8] for s, i in sources])
        total = functools.reduce(jnp.add, [refs[s][i, 8:16] for s, i in sources])
        top = jnp.max(top, 0, keepdims=True)
        total = jnp.sum(total, 0, keepdims=True)
        for half in range(2):
            first, second = steps[2 * chunk + half]
            to_x = lax.rem(x + jnp.where(straight, first, second) + NX, NX)
            to_y = lax.rem(y + jnp.where(straight, second, first) + NY, NY)
            place = (to_x * NY + to_y) * 2
            out_ref[pl.ds(place, 1), :] = top[:, 128 * half : 128 * half + 128]
            out_ref[pl.ds(place + 1, 1), :] = total[:, 128 * half : 128 * half + 128]


def collect(plan, steps, stages):
    return pl.pallas_call(
        functools.partial(collect_kernel, plan, steps),
        out_shape=f32(2 * NX * NY, 128),
        in_specs=[VM] * len(stages),
        out_specs=VM,
        compiler_params=SMALL,
        name="collect",
    )(*stages)


def finish_kernel(parts_ref, top_ref, soft_ref):
    top = parts_ref[0:1, :]
    total = parts_ref[1:2, :]
    for i in range(1, NX * NY):
        top = jnp.maximum(top, parts_ref[2 * i : 2 * i + 1, :])
        total = total + parts_ref[2 * i + 1 : 2 * i + 2, :]
    top_ref[...] = (top + OFFSET * LOG2E) * (1.0 / LOG2E)
    soft_ref[...] = jnp.log1p(total)


def finish(parts):
    return pl.pallas_call(
        finish_kernel,
        out_shape=(f32(1, ROWS), f32(1, ROWS)),
        in_specs=[VM],
        out_specs=(VM, VM),
        compiler_params=SMALL,
        name="finish",
    )(parts)


def per_device(rows, mark):
    together = lax.optimization_barrier
    mine = prepare(rows, mark)
    keys = lambda first, second: pack(pack_keys_kernel, "pack_keys", PAIR, first, second)
    a = first_axis(mine, 1)
    b = first_axis(mine, -1)
    d = first_axis(mine, 2)
    other = swap(mine)
    z0 = keys(mine, other)
    t1 = away(z0)
    x = pack(pack_queries_kernel, "pack_line", 2 * PAIR, mine, d, a, b)
    e = second_axis(x, 1)
    f = second_axis(x, -1)
    s0 = stage([x], [z0], ((0,),) * 2, True, "stage_0", 3000000000)
    t1, s0 = together((t1, s0))
    t2 = away(t1)
    u1 = swap(t1)
    s1 = stage([x], [t1], ((0,),) * 2, False, "stage_1", 10000000000)
    t2, u1, s1 = together((t2, u1, s1))

    t3 = away(t2)
    u2 = swap(t2)
    s2 = stage([x], [t2, u1, u2], ((0, 1, 2),) * 2, False, "stage_2", 0)
    e, f, s2 = together((e, f, s2))

    g1 = second_axis(pack(functools.partial(half_queries_kernel, 0), "half_near", PAIR, e), 1)
    g2 = second_axis(pack(functools.partial(half_queries_kernel, 1), "half_far", PAIR, f), -1)
    s3 = stage([e], [z0, t1, u1, t2, u2], ((0, 1, 2, 3, 4),) * 2, False, "stage_3", 0)
    t3, s3 = together((t3, s3))

    t4 = away(pack(first_half_kernel, "first_half", ROWS, t3))
    s4 = stage([f], [z0, t1, u1, t2, u2], ((0, 1, 2, 3, 4),) * 2, False, "stage_4", 0)
    t3, s4 = together((t3, s4))
    u3 = swap(t3)
    s4b = stage([x, e, f], [t3], ((0,),) * 6, False, "stage_4b")
    g1, g2, s4, s4b = together((g1, g2, s4, s4b))
    s5 = stage([g1, g2], [z0, t1, u1, t2, u2, t3], ((0, 1, 2, 3, 4, 5),) * 2, False, "stage_5", 0)
    t4, s5 = together((t4, s5))
    queries = [x, e, f, g1, g2]
    u4 = swap(t4)
    s6 = stage(queries, [u3], ((0,),) * 8, False, "stage_6")
    s7 = stage(queries, [keys(t4, u4)], ((0,),) * 8, False, "stage_7")

    near, far = ((0, 0), (-2, 0)), ((-1, 0), (1, 0))
    move = lambda pair, step: tuple((p, step) for p, _ in pair)
    chunks = [near, far, move(near, -1), move(far, -1), move(near, 1), move(far, 1), move(near, -2), move(far, 2)]
    steps = [s for pair in chunks for s in pair]
    stages = [s0, s1, s2, s3, s4, s4b, s5, s6, s7]
    held = [(0, 1), (0, 1), (0, 1), (2, 3), (4, 5), range(6), (6, 7), range(8), range(8)]
    plan = [[(i, list(h).index(q)) for i, h in enumerate(held) if q in h] for q in range(8)]

    parts = collect(plan, steps, stages)
    parts = lax.all_to_all(parts, ("x", "y"), split_axis=0, concat_axis=0, tiled=True)
    top, soft = finish(parts)
    return top.reshape(ROWS), soft.reshape(ROWS)


def solution(mesh):
    fine = Mesh(mesh.devices.reshape(NX, NZ, NY, NC), AXES)
    return jax.shard_map(
        per_device,
        mesh=fine,
        in_specs=(P(AXES, None), P(AXES, None)),
        out_specs=(P(AXES), P(AXES)),
        check_vma=False,
    )
```
